32 devices in a mesh: group: 2 (over y), tensor: 16 (over z, x, core).
Axes of the slice: x: 2, y: 2, z: 4, core: 2. Of those that a mesh axis runs over, the one named last changes fastest.
Arguments:
- tokens: bfloat16 [512, 8192], P('group', 'tensor'), parts along dimension 0, may hold values from -480 to 480, as said below
- norm_gain: float32 [8192], replicated, may hold values from 0.5 to 1.5
- gate_levels: bfloat16 [8192, 26624], P(None, 'tensor'), may hold values from -8 to 7, as said below
- gate_scale: float32 [26624], P('tensor'), may hold values from 0.0012 to 0.0048
- up_levels: bfloat16 [8192, 26624], P(None, 'tensor'), may hold values from -8 to 7, as said below
- up_scale: float32 [26624], P('tensor'), may hold values from 0.0012 to 0.0048
- odd_factor: float32 [13, 13], replicated, may hold values from -1.75 to 1.75
- down_levels: bfloat16 [26624, 8192], P('tensor'), may hold values from -8 to 7, as said below
- down_scale: float32 [8192], P('tensor'), may hold values from 0.0013 to 0.005
Outputs:
- mixed: bfloat16 [512, 8192], P('group', 'tensor'), parts along dimension 0
The draws below stay inside these ranges and needn't reach their ends.
There are 2 independent parts, one for each index of `group`. The reference program is written for one: setup_inputs(seed, part) draws one part's arguments, and reference() takes and returns one part's arrays. A program takes and returns all parts, laid end to end along the dimension named above; an argument that names none is the same for every part. Nothing has to cross between parts.
Inputs may be any that keep to these rules, and one draw needn't show every extreme that they name: `tokens`: row and column scales vary. `gate_levels`: whole numbers. `up_levels`: whole numbers. `down_levels`: whole numbers.
All inputs are finite; a program needn't handle non-finite values.
Results may differ from the reference program's by a relative error of at most 0.0071.
Values may be sent and summed in bfloat16 or wider, within the bound.
A program may use at most 384 MiB of HBM per device.

```python
import math
import jax
import jax.numpy as jnp
from jax import lax

D = 8192
FF = 26624
ODD = 13
WAL = 2048
ROWS = 256


def draw_tokens(key, part):
    key = jax.random.fold_in(key, 11)
    first_key, second_key, third_key = jax.random.split(key, 3)
    columns = jnp.arange(D, dtype=jnp.float32) / D
    noise = jnp.clip(jax.random.normal(first_key, (ROWS, D), jnp.float32), -4.0, 4.0)
    column_scale = jnp.exp(math.log(3.0) * columns + jax.random.uniform(second_key, (D,), jnp.float32, 0.0, math.log(3.3)))
    row_scale = jnp.exp(jax.random.uniform(third_key, (ROWS, 1), jnp.float32, 0.0, math.log(10.0)))
    return (noise * row_scale * column_scale).astype(jnp.bfloat16)


def draw_gate_levels(key, part):
    key = jax.random.fold_in(key, 21)
    levels = jax.random.randint(key, (D, FF), -8, 8, jnp.int32)
    return levels.astype(jnp.float32).astype(jnp.bfloat16)


def draw_up_levels(key, part):
    key = jax.random.fold_in(key, 31)
    levels = jax.random.randint(key, (D, FF), -8, 8, jnp.int32)
    return levels.astype(jnp.float32).astype(jnp.bfloat16)


def draw_down_levels(key, part):
    key = jax.random.fold_in(key, 41)
    levels = jax.random.randint(key, (FF, D), -8, 8, jnp.int32)
    return levels.astype(jnp.float32).astype(jnp.bfloat16)


def steps_of(rng, shape, cuts, least, top_value):
    level, own = 1.0, jax.random.fold_in(rng, 6)
    for position, parts in cuts:
        steps = jnp.exp(jax.random.uniform(jax.random.fold_in(own, position), (parts,), jnp.float32, least / len(cuts), top_value / len(cuts)))
        level = level * jnp.repeat(steps, shape[position] // parts).reshape([-1 if axis == position else 1 for axis in range(len(shape))])
    return level


def centred(rng, extent, spread, reach, kind=jnp.bfloat16):
    entries = spread * jax.random.normal(rng, extent, jnp.float32)
    return jnp.clip(entries, min=-reach, max=reach).astype(kind)


def setup_inputs(seed: int = 0, part: int = 0) -> dict:
    keys = jax.random.split(jax.random.key(seed), 10)
    part_splits = jax.random.split(jax.random.fold_in(keys[9], part), 10)
    tokens = draw_tokens(jax.random.fold_in(jax.random.fold_in(keys[9], part), 71), part)
    norm_gain = jnp.clip(1.0 + 0.1 * jax.random.normal(keys[1], (D,), jnp.float32), 0.5, 1.5)
    gate_levels = draw_gate_levels(jax.random.fold_in(keys[9], 71), part)
    gate_scale = jnp.clip(jnp.exp(math.log(0.0048) - 1.3862944 * jax.random.uniform(keys[3], (FF,), jnp.float32) ** steps_of(keys[3], (FF,), ((0, 16),), -0.2, 0.2)), 0.0012, 0.0048)
    up_levels = draw_up_levels(jax.random.fold_in(keys[9], 71), part)
    up_scale = jnp.clip(jnp.exp(math.log(0.0048) - 1.3862944 * jax.random.uniform(keys[5], (FF,), jnp.float32) ** steps_of(keys[5], (FF,), ((0, 16),), -0.2, 0.2)), 0.0012, 0.0048)
    odd_factor = centred(keys[6], (ODD, ODD), ODD ** -0.5, 1.75, jnp.float32)
    down_levels = draw_down_levels(jax.random.fold_in(keys[9], 71), part)
    down_scale = jnp.clip(jnp.exp(math.log(0.005) - 1.34707362 * jax.random.uniform(keys[8], (D,), jnp.float32) ** steps_of(keys[8], (D,), ((0, 16),), -0.2, 0.2)), 0.0013, 0.005)
    return {"tokens": tokens, "norm_gain": norm_gain, "gate_levels": gate_levels, "gate_scale": gate_scale, "up_levels": up_levels, "up_scale": up_scale, "odd_factor": odd_factor, "down_levels": down_levels, "down_scale": down_scale}


def walsh_rows(grouped):
    row_count, order, inner = grouped.shape
    stride = 1
    while stride < order:
        shaped = grouped.reshape(row_count, order // (2 * stride), 2, stride, inner)
        first_half = shaped[:, :, 0]
        second_half = shaped[:, :, 1]
        grouped = jnp.stack([first_half + second_half, first_half - second_half], axis=2).reshape(row_count, order, inner)
        stride = stride * 2
    return grouped

def reference(tokens, norm_gain, gate_levels, gate_scale, up_levels, up_scale, odd_factor, down_levels, down_scale):
    floats = tokens.astype(jnp.float32)
    inverse = lax.rsqrt(lax.optimization_barrier(jnp.mean(floats * floats, axis=1, keepdims=True)) + 1e-05)
    normed = (floats * inverse * norm_gain).astype(jnp.bfloat16)
    gate_out = jnp.dot(normed, gate_levels, preferred_element_type=jnp.float32) * gate_scale
    up_out = jnp.dot(normed, up_levels, preferred_element_type=jnp.float32) * up_scale
    hidden = (jax.nn.silu(gate_out) * up_out).astype(jnp.bfloat16)
    row_count = hidden.shape[0]
    grouped = hidden.astype(jnp.float32).reshape(row_count, WAL, ODD)
    grouped = jnp.einsum('rwj,kj->rwk', grouped, odd_factor, precision=lax.Precision.HIGHEST)
    grouped = walsh_rows(grouped)
    rotated = (grouped.reshape(row_count, FF) * (1.0 / math.sqrt(WAL))).astype(jnp.bfloat16)
    summed = jnp.dot(rotated, down_levels, preferred_element_type=jnp.float32)
    return (summed * down_scale).astype(jnp.bfloat16)
```

```python
import functools
import math

import jax
import jax.numpy as jnp
import numpy as np
from jax import lax
from jax.experimental import pallas as pl
from jax.experimental.pallas import tpu as pltpu
from jax.sharding import PartitionSpec as P

F32 = jnp.float32
BF16 = jnp.bfloat16
MESH = pl.DeviceIdType.MESH

ORDER = (0, 2, 4, 8, 6, 12, 10, 14)
ONWARD = (
    ((0, 8), (0, 4), (0, 2), (0, 1)),
    ((2, 1),),
    ((4, 2), (4, 1)),
    ((8, 4), (8, 2), (8, 1)),
    ((6, 1),),
    ((12, 2), (12, 1)),
    ((10, 1),),
    ((14, 1),),
)
RING = 5
DOWN_RING = 8


def pick(index, table):
    value = jnp.int32(table[0])
    for place, entry in enumerate(table[1:], 1):
        value = jnp.where(index == place, jnp.int32(entry), value)
    return value


def fused_kernel(
    n,
    odd_order,
    splits,
    walsh_scale,
    tokens,
    gain,
    gate_hbm,
    gate_scale,
    up_hbm,
    up_scale,
    odd_t,
    down_hbm,
    down_scale,
    ones_row,
    ones_col,
    sign_row,
    sign_col,
    out,
    tok,
    square,
    gate_w,
    up_w,
    down_w,
    gate_acc,
    up_acc,
    mixer,
    hid,
    arrived,
    rot_out,
    rot_in,
    kept,
    core_out,
    core_in,
    x_out,
    x_in,
    z_out,
    z_in,
    gate_sem,
    up_sem,
    down_sem,
    tok_send,
    tok_recv,
    hid_send,
    hid_recv,
    rot_send,
    rot_recv,
    core_send,
    core_recv,
    x_send,
    x_recv,
    z_send,
    z_recv,
):
    me = lax.axis_index("tensor")
    rows, depth = tokens.shape
    width = gate_acc.shape[1]
    share = rows // n
    steps = 2 * len(ORDER)

    def remote(source, target, offset, send, recv):
        return pltpu.make_async_remote_copy(
            src_ref=source,
            dst_ref=target,
            send_sem=send,
            recv_sem=recv,
            device_id={"tensor": jnp.bitwise_xor(me, offset)},
            device_id_type=MESH,
        )

    def weight_copies(step):
        offset = pick(step // 2, ORDER) + step % 2
        start = pl.multiple_of(jnp.bitwise_xor(me, offset) * depth, depth)
        slot = lax.rem(step, RING)
        return (
            pltpu.make_async_copy(gate_hbm.at[pl.ds(start, depth), :], gate_w.at[slot], gate_sem.at[slot]),
            pltpu.make_async_copy(up_hbm.at[pl.ds(start, depth), :], up_w.at[slot], up_sem.at[slot]),
        )

    def start_weights(step, carry=None):
        for copy in weight_copies(step):
            copy.start()
        return carry

    def down_copy(step):
        owner = jnp.bitwise_xor(me, steps - 1 - step)
        start = pl.multiple_of(owner * depth, depth)
        slot = lax.rem(step, DOWN_RING)
        return pltpu.make_async_copy(down_hbm.at[:, pl.ds(start, depth)], down_w.at[slot], down_sem.at[slot])

    lax.fori_loop(0, RING, lambda s, c: start_weights(jnp.int32(s), c), 0)

    barrier = pltpu.get_barrier_semaphore()

    def greet(offset, carry):
        pl.semaphore_signal(
            barrier, inc=1, device_id={"tensor": jnp.bitwise_xor(me, offset)}, device_id_type=MESH
        )
        return carry

    lax.fori_loop(1, n, greet, 0)
    tok[0] = tokens[...]
    pl.semaphore_wait(barrier, n - 1)

    def pass_on(block, offset):
        landing = block ^ offset
        return remote(tok.at[block], tok.at[landing], offset, tok_send.at[landing], tok_recv.at[landing])

    def wait_block(landing):
        remote(tok.at[landing], tok.at[landing], 1, tok_send.at[landing], tok_recv.at[landing]).wait_recv()

    for block, offset in ONWARD[0]:
        pass_on(block, offset).start()

    def build(tile, carry):
        at = pl.ds(pl.multiple_of(tile * 128, 128), 128)
        factor_rows = jnp.dot(ones_row[at, :], odd_t[...], preferred_element_type=F32).astype(BF16)
        factor = jnp.dot(factor_rows, ones_col[...], preferred_element_type=F32)
        signs = jnp.dot(sign_row[at, :], sign_col[...], preferred_element_type=F32)
        mixer[at, :] = (factor * signs).astype(BF16)
        return carry

    lax.fori_loop(0, width // 128, build, 0)
    square[...] = jnp.zeros_like(square)
    gate_acc[...] = jnp.zeros_like(gate_acc)
    up_acc[...] = jnp.zeros_like(up_acc)

    def project(step, carry):
        pair, side = step // 2, step % 2
        for place, moves in enumerate(ONWARD):
            if place > 0:

                @pl.when((pair == place) & (side == 0))
                def _(moves=moves):
                    wait_block(moves[0][0])
                    for block, offset in moves:
                        pass_on(block, offset).start()

        offset = pick(pair, ORDER) + side

        @pl.when(side == 1)
        def _():
            wait_block(offset)

        for copy in weight_copies(step):
            copy.wait()
        slot = lax.rem(step, RING)
        block = tok[offset].astype(F32)
        part = square[...]
        for lane in range(0, depth, 128):
            piece = block[:, lane : lane + 128]
            part = part + piece * piece
        square[...] = part
        scaled = (block * gain[jnp.bitwise_xor(me, offset)]).astype(BF16)
        gate_acc[...] += jnp.dot(scaled, gate_w[slot], preferred_element_type=F32)
        up_acc[...] += jnp.dot(scaled, up_w[slot], preferred_element_type=F32)

        @pl.when(step + RING < steps)
        def _():
            start_weights(step + RING)

        return carry

    lax.fori_loop(0, steps, project, 0)

    def start_down(step, carry):
        down_copy(step).start()
        return carry

    lax.fori_loop(0, DOWN_RING, lambda s, c: start_down(jnp.int32(s), c), 0)

    def rows_of(device):
        return pl.ds(pl.multiple_of(device * share, share), share)

    def exchange(source, target, part, offset, send, recv):
        first, size = splits[part]
        cut = pl.ds(first, size)
        peer = jnp.bitwise_xor(me, offset)
        return remote(
            source.at[rows_of(peer), cut],
            target.at[rows_of(me), cut],
            offset,
            send.at[part, offset],
            recv.at[part, offset],
        )

    def each_peer(act):
        def one(index, carry):
            act(n - index)
            return carry

        lax.fori_loop(1, n, one, 0)

    mean = jnp.sum(square[...], axis=1, keepdims=True) * (1.0 / (n * depth))
    inverse = lax.rsqrt(mean + 1e-05)

    for part, (first, size) in enumerate(splits):

        def activate(tile, carry, first=first):
            at = pl.ds(pl.multiple_of(first + tile * 128, 128), 128)
            gate = gate_acc[:, at] * inverse * gate_scale[:, at]
            up = up_acc[:, at] * inverse * up_scale[:, at]
            hid[:, at] = (gate / (1.0 + jnp.exp(-gate)) * up).astype(BF16)
            return carry

        lax.fori_loop(0, size // 128, activate, 0)
        each_peer(lambda j, part=part: exchange(hid, arrived, part, j, hid_send, hid_recv).start())
    arrived[rows_of(me), :] = hid[rows_of(me), :]
    for part in range(len(splits)):
        each_peer(lambda j, part=part: exchange(hid, arrived, part, j, hid_send, hid_recv).wait_recv())

    def mix(first, size):
        at = pl.ds(first, size)
        flat = jnp.dot(arrived[...], mixer[:, at], preferred_element_type=F32)
        terms = [flat[i * share : (i + 1) * share] for i in range(n)]
        bit = 1
        while bit < n:
            terms = [
                terms[i ^ bit] - terms[i] if i & bit else terms[i] + terms[i ^ bit] for i in range(n)
            ]
            bit *= 2
        for i in range(n):
            rot_out[i * share : (i + 1) * share, at] = (terms[i] * walsh_scale).astype(BF16)

    for part, (first, size) in enumerate(splits):

        def mix_tile(tile, carry, first=first):
            mix(pl.multiple_of(first + tile * 256, 256), 256)
            return carry

        lax.fori_loop(0, size // 256, mix_tile, 0)
        if size % 256:
            mix(first + size // 256 * 256, size % 256)
        each_peer(lambda j, part=part: exchange(rot_out, rot_in, part, j, rot_send, rot_recv).start())
    rot_in[rows_of(me), :] = rot_out[rows_of(me), :]
    for part in range(len(splits)):
        each_peer(lambda j, part=part: exchange(rot_out, rot_in, part, j, rot_send, rot_recv).wait_recv())

    groups = steps // 2

    def down_block(step):
        down_copy(step).wait()
        value = jnp.dot(rot_in[...], down_w[lax.rem(step, DOWN_RING)], preferred_element_type=F32)
        return value

    def refill(step):
        @pl.when(step + DOWN_RING < steps)
        def _():
            down_copy(step + DOWN_RING).start()

    def to_core(group):
        return remote(core_out.at[group], core_in.at[group], 1, core_send.at[group], core_recv.at[group])

    def to_x(turn):
        return remote(x_out.at[turn], x_in.at[turn], 2, x_send.at[turn], x_recv.at[turn])

    def to_z(turn, offset):
        return remote(z_out.at[turn], z_in.at[turn], offset, z_send.at[turn], z_recv.at[turn])

    def combine(group):
        to_core(group).wait_recv()
        total = kept[group] + core_in[group].astype(F32)
        turn = group // 2

        @pl.when(group % 2 == 0)
        def _():
            x_out[turn] = total.astype(BF16)
            to_x(turn).start()

        @pl.when(group % 2 == 1)
        def _():
            kept[group] = total

    def lower(group, carry):
        core_out[group] = down_block(2 * group).astype(BF16)
        to_core(group).start()
        refill(2 * group)
        kept[group] = down_block(2 * group + 1)
        refill(2 * group + 1)

        @pl.when(group > 0)
        def _():
            combine(group - 1)

        return carry

    lax.fori_loop(0, groups, lambda g, c: lower(jnp.int32(g), c), 0)
    combine(jnp.int32(groups - 1))

    to_x(0).wait_recv()
    z_out[0] = (kept[1] + x_in[0].astype(F32)).astype(BF16)
    to_z(0, 4).start()
    to_x(1).wait_recv()
    to_z(0, 4).wait_recv()
    z_out[1] = (kept[3] + x_in[1].astype(F32) + z_in[0].astype(F32)).astype(BF16)
    to_z(1, 8).start()
    to_x(2).wait_recv()
    z_out[2] = (kept[5] + x_in[2].astype(F32)).astype(BF16)
    to_z(2, 4).start()
    to_x(3).wait_recv()
    to_z(1, 8).wait_recv()
    total = kept[7] + x_in[3].astype(F32) + z_in[1].astype(F32)
    to_z(2, 4).wait_recv()
    out[...] = ((total + z_in[2].astype(F32)) * down_scale[...]).astype(BF16)

    for moves in ONWARD:
        for block, offset in moves:
            pass_on(block, offset).wait_send()
    for part in range(len(splits)):
        each_peer(lambda j, part=part: exchange(hid, arrived, part, j, hid_send, hid_recv).wait_send())
        each_peer(lambda j, part=part: exchange(rot_out, rot_in, part, j, rot_send, rot_recv).wait_send())

    def finish(group, carry):
        to_core(group).wait_send()
        return carry

    lax.fori_loop(0, groups, finish, 0)
    for turn in range(4):
        to_x(turn).wait_send()
    for turn, offset in ((0, 4), (1, 8), (2, 4)):
        to_z(turn, offset).wait_send()


def small_signs(order):
    indices = np.arange(order)
    common = indices[:, None] & indices[None, :]
    parity = np.zeros_like(common)
    while common.any():
        parity ^= common & 1
        common >>= 1
    return 1.0 - 2.0 * parity


def fused_shards(
    tokens,
    norm_gain,
    gate_levels,
    gate_scale,
    up_levels,
    up_scale,
    odd_factor,
    down_levels,
    down_scale,
):
    n = lax.axis_size("tensor")
    rows, depth = tokens.shape
    width = gate_levels.shape[1]
    odd_order = odd_factor.shape[0]
    order = width // odd_order
    units = np.arange(width)
    ones = np.zeros((width, 128), np.float32)
    ones[units, units % odd_order] = 1.0
    owners = np.zeros((width, order), np.float32)
    owners[units, units // odd_order] = 1.0
    signs = owners @ small_signs(order)
    constants = [jnp.asarray(a, BF16) for a in (ones, ones.T, signs, owners.T)]
    odd_t = jnp.pad(odd_factor.T, ((0, 128 - odd_order),) * 2).astype(BF16)
    half = width // 2 // 256 * 256
    splits = ((0, half), (half, width - half))
    vmem = pl.BlockSpec(memory_space=pltpu.VMEM)
    hbm = pl.BlockSpec(memory_space=pl.ANY)
    dma = pltpu.SemaphoreType.DMA
    block = (rows, depth)
    kernel = functools.partial(fused_kernel, n, odd_order, splits, 1.0 / math.sqrt(order * n))
    return pl.pallas_call(
        kernel,
        out_shape=jax.ShapeDtypeStruct(block, BF16),
        in_specs=[vmem, vmem, hbm, vmem, hbm, vmem, vmem, hbm, vmem] + [vmem] * 4,
        out_specs=vmem,
        scratch_shapes=[
            pltpu.VMEM((n,) + block, BF16),
            pltpu.VMEM((rows, 128), F32),
            pltpu.VMEM((RING, depth, width), BF16),
            pltpu.VMEM((RING, depth, width), BF16),
            pltpu.VMEM((DOWN_RING, width, depth), BF16),
            pltpu.VMEM((rows, width), F32),
            pltpu.VMEM((rows, width), F32),
            pltpu.VMEM((width, width), BF16),
            pltpu.VMEM((rows, width), BF16),
            pltpu.VMEM((rows, width), BF16),
            pltpu.VMEM((rows, width), BF16),
            pltpu.VMEM((rows, width), BF16),
            pltpu.VMEM((8,) + block, F32),
            pltpu.VMEM((8,) + block, BF16),
            pltpu.VMEM((8,) + block, BF16),
            pltpu.VMEM((4,) + block, BF16),
            pltpu.VMEM((4,) + block, BF16),
            pltpu.VMEM((3,) + block, BF16),
            pltpu.VMEM((3,) + block, BF16),
            dma((RING,)),
            dma((RING,)),
            dma((DOWN_RING,)),
            dma((n,)),
            dma((n,)),
            dma((2, n)),
            dma((2, n)),
            dma((2, n)),
            dma((2, n)),
            dma((8,)),
            dma((8,)),
            dma((4,)),
            dma((4,)),
            dma((3,)),
            dma((3,)),
        ],
        compiler_params=pltpu.CompilerParams(
            collective_id=0, has_side_effects=True, vmem_limit_bytes=64 * 1024 * 1024 - 65536
        ),
        cost_estimate=pl.CostEstimate(
            flops=2 * rows * width * (3 * n * depth + width),
            bytes_accessed=6 * n * depth * width,
            transcendentals=rows * width,
        ),
    )(
        tokens,
        norm_gain.reshape(n, 1, depth),
        gate_levels,
        gate_scale.reshape(1, width),
        up_levels,
        up_scale.reshape(1, width),
        odd_t,
        down_levels,
        down_scale.reshape(1, depth),
        *constants,
    )


def partner_2(block, axis, distance):
    count = lax.axis_size(axis)
    route = []
    for low in range(count):
        high = low | 1 << distance
        if high != low and high < count:
            route += [(low, high), (high, low)]
    return lax.ppermute(block, axis, route)


def sign_table(order):
    indices = jnp.arange(order, dtype=jnp.int32)
    common_bits = jnp.bitwise_and(indices[:, None], indices[None, :])
    parity = jnp.zeros((order, order), jnp.int32)
    for bit_index in range(max(1, order.bit_length())):
        parity = parity + jnp.bitwise_and(jnp.right_shift(common_bits, bit_index), 1)
    return (1 - 2 * jnp.bitwise_and(parity, 1)).astype(jnp.float32)


def shards(
    tokens,
    norm_gain,
    gate_levels,
    gate_scale,
    up_levels,
    up_scale,
    odd_factor,
    down_levels,
    down_scale,
):
    devices = lax.axis_size("tensor")
    order = gate_levels.shape[1] // odd_factor.shape[0]
    if devices == 16 and order == 128 and tokens.shape[1] % 128 == 0 and tokens.shape[0] % 256 == 0:
        return fused_shards(
            tokens,
            norm_gain,
            gate_levels,
            gate_scale,
            up_levels,
            up_scale,
            odd_factor,
            down_levels,
            down_scale,
        )
    gathered = lax.all_gather(tokens, "tensor", axis=1, tiled=True)
    floats = gathered.astype(jnp.float32)
    inverse = lax.rsqrt(jnp.mean(floats * floats, axis=1, keepdims=True) + 1e-05)
    normed = (floats * inverse * norm_gain).astype(jnp.bfloat16)
    gate_out = jnp.dot(normed, gate_levels, preferred_element_type=jnp.float32) * gate_scale
    up_out = jnp.dot(normed, up_levels, preferred_element_type=jnp.float32) * up_scale
    hidden = (jax.nn.silu(gate_out) * up_out).astype(jnp.bfloat16)
    odd_order = odd_factor.shape[0]
    hidden_width = hidden.shape[1]
    local_order = hidden_width // odd_order
    local_mixer = jnp.kron(sign_table(local_order), odd_factor.T)
    spread = jnp.dot(hidden.astype(jnp.float32), local_mixer, precision=lax.Precision.HIGHEST)
    position = lax.axis_index("tensor")
    for bit_index in range(devices.bit_length() - 1):
        partner = partner_2(spread, "tensor", bit_index)
        is_upper = jnp.bitwise_and(jnp.right_shift(position, bit_index), 1) == 1
        spread = jnp.where(is_upper, partner - spread, spread + partner)
    walsh_scale = 1.0 / math.sqrt(local_order * devices)
    rotated = (spread * walsh_scale).astype(jnp.bfloat16)
    partials = jnp.dot(rotated, down_levels, preferred_element_type=jnp.float32)
    summed = lax.psum_scatter(partials, "tensor", scatter_dimension=1, tiled=True)
    return (summed * down_scale).astype(jnp.bfloat16)


def solution(mesh):
    placed = (
        P("group", "tensor"),
        P(),
        P(None, "tensor"),
        P("tensor"),
        P(None, "tensor"),
        P("tensor"),
        P(),
        P("tensor", None),
        P("tensor"),
    )
    return jax.shard_map(
        shards, mesh=mesh, in_specs=placed, out_specs=P("group", "tensor"), check_vma=False
    )
```

```python
import functools
import math

import jax
import jax.numpy as jnp
import numpy as np
from jax import lax
from jax.experimental import pallas as pl
from jax.experimental.pallas import tpu as pltpu
from jax.sharding import PartitionSpec as P

F32 = jnp.float32
BF16 = jnp.bfloat16
MESH = pl.DeviceIdType.MESH

ORDER = (0, 2, 4, 8, 6, 12, 10, 14)
ONWARD = (
    ((0, 8), (0, 4), (0, 2), (0, 1)),
    ((2, 1),),
    ((4, 2), (4, 1)),
    ((8, 4), (8, 2), (8, 1)),
    ((6, 1),),
    ((12, 2), (12, 1)),
    ((10, 1),),
    ((14, 1),),
)
RING = 5
DOWN_RING = 8


def pick(index, table):
    value = jnp.int32(table[0])
    for place, entry in enumerate(table[1:], 1):
        value = jnp.where(index == place, jnp.int32(entry), value)
    return value


def fused_kernel(
    n,
    odd_order,
    splits,
    walsh_scale,
    tokens,
    gain,
    gate_hbm,
    gate_scale_1d,
    up_hbm,
    up_scale_1d,
    odd,
    down_hbm,
    down_scale,
    ones_row_hbm,
    ones_col_hbm,
    sign_row_hbm,
    sign_col_hbm,
    out,
    tok,
    inverse,
    gate_scale,
    up_scale,
    sums,
    odd_pad,
    ones_row,
    ones_col,
    sign_row,
    sign_col,
    gate_w,
    up_w,
    down_w,
    gate_acc,
    up_acc,
    mixer,
    hid,
    arrived,
    rot_out,
    rot_in,
    kept,
    core_out,
    core_in,
    x_out,
    x_in,
    z_out,
    z_in,
    gate_sem,
    up_sem,
    down_sem,
    sums_send,
    sums_recv,
    const_sem,
    tok_send,
    tok_recv,
    hid_send,
    hid_recv,
    rot_send,
    rot_recv,
    core_send,
    core_recv,
    x_send,
    x_recv,
    z_send,
    z_recv,
):
    me = lax.axis_index("tensor")
    rows, depth = tokens.shape
    width = gate_acc.shape[1]
    share = rows // n
    steps = 2 * len(ORDER)

    def remote(source, target, offset, send, recv):
        return pltpu.make_async_remote_copy(
            src_ref=source,
            dst_ref=target,
            send_sem=send,
            recv_sem=recv,
            device_id={"tensor": jnp.bitwise_xor(me, offset)},
            device_id_type=MESH,
        )

    def weight_copies(step):
        offset = pick(step // 2, ORDER) + step % 2
        start = pl.multiple_of(jnp.bitwise_xor(me, offset) * depth, depth)
        slot = lax.rem(step, RING)
        return (
            pltpu.make_async_copy(gate_hbm.at[pl.ds(start, depth), :], gate_w.at[slot], gate_sem.at[slot]),
            pltpu.make_async_copy(up_hbm.at[pl.ds(start, depth), :], up_w.at[slot], up_sem.at[slot]),
        )

    def start_weights(step, carry=None):
        for copy in weight_copies(step):
            copy.start()
        return carry

    def down_copy(step):
        owner = jnp.bitwise_xor(me, steps - 1 - step)
        start = pl.multiple_of(owner * depth, depth)
        slot = lax.rem(step, DOWN_RING)
        return pltpu.make_async_copy(down_hbm.at[:, pl.ds(start, depth)], down_w.at[slot], down_sem.at[slot])

    lax.fori_loop(0, RING, lambda s, c: start_weights(jnp.int32(s), c), 0)

    constant_copies = [
        pltpu.make_async_copy(source, target, const_sem.at[i])
        for i, (source, target) in enumerate(
            (
                (ones_row_hbm, ones_row),
                (ones_col_hbm, ones_col),
                (sign_row_hbm, sign_row),
                (sign_col_hbm, sign_col),
            )
        )
    ]
    for copy in constant_copies:
        copy.start()

    barrier = pltpu.get_barrier_semaphore()

    def greet(offset, carry):
        pl.semaphore_signal(
            barrier, inc=1, device_id={"tensor": jnp.bitwise_xor(me, offset)}, device_id_type=MESH
        )
        return carry

    lax.fori_loop(1, n, greet, 0)
    tok[0] = tokens[...]
    own = tokens[...].astype(F32)
    part = jnp.zeros((rows, 128), F32)
    for lane in range(0, depth, 128):
        part = part + own[:, lane : lane + 128] * own[:, lane : lane + 128]
    sums[0] = lax.dot_general(
        jnp.ones((8, 128), F32),
        part,
        (((1,), (1,)), ((), ())),
        precision=lax.Precision.HIGHEST,
        preferred_element_type=F32,
    )
    pl.semaphore_wait(barrier, n - 1)

    def pass_on(block, offset):
        landing = block ^ offset
        return remote(tok.at[block], tok.at[landing], offset, tok_send.at[landing], tok_recv.at[landing])

    def wait_block(landing):
        remote(tok.at[landing], tok.at[landing], 1, tok_send.at[landing], tok_recv.at[landing]).wait_recv()

    def sums_to(j):
        return remote(sums.at[0], sums.at[j], j, sums_send.at[j], sums_recv.at[j])

    def each_peer(act):
        def one(index, carry):
            act(n - index)
            return carry

        lax.fori_loop(1, n, one, 0)

    each_peer(lambda j: sums_to(j).start())
    for block, offset in ONWARD[0]:
        pass_on(block, offset).start()
    gate_scale[...] = gate_scale_1d[...].reshape(1, width)
    up_scale[...] = up_scale_1d[...].reshape(1, width)

    gate_acc[...] = jnp.zeros_like(gate_acc)
    up_acc[...] = jnp.zeros_like(up_acc)

    each_peer(lambda j: sums_to(j).wait_recv())
    total = sums[0]
    for j in range(1, n):
        total = total + sums[j]
    spread = lax.dot_general(
        total,
        jnp.full((8, 128), 0.125, F32),
        (((0,), (0,)), ((), ())),
        precision=lax.Precision.HIGHEST,
        preferred_element_type=F32,
    )
    inverse[...] = lax.rsqrt(spread * (1.0 / (n * depth)) + 1e-05)

    def project(step, carry):
        pair, side = step // 2, step % 2
        for place, moves in enumerate(ONWARD):
            if place > 0:

                @pl.when((pair == place) & (side == 0))
                def _(moves=moves):
                    wait_block(moves[0][0])
                    for block, offset in moves:
                        pass_on(block, offset).start()

        offset = pick(pair, ORDER) + side

        @pl.when(side == 1)
        def _():
            wait_block(offset)

        for copy in weight_copies(step):
            copy.wait()
        slot = lax.rem(step, RING)
        block = tok[offset].astype(F32)
        factor = jnp.concatenate([inverse[...]] * (depth // 128), axis=1)
        scaled = (block * factor * gain[jnp.bitwise_xor(me, offset)]).astype(BF16)
        gate_acc[...] += jnp.dot(scaled, gate_w[slot], preferred_element_type=F32)
        up_acc[...] += jnp.dot(scaled, up_w[slot], preferred_element_type=F32)

        @pl.when(step + RING < steps)
        def _():
            start_weights(step + RING)

        return carry

    lax.fori_loop(0, steps, project, 0)

    def start_down(step, carry):
        down_copy(step).start()
        return carry

    lax.fori_loop(0, DOWN_RING, lambda s, c: start_down(jnp.int32(s), c), 0)

    def rows_of(device):
        return pl.ds(pl.multiple_of(device * share, share), share)

    def exchange(source, target, part, offset, send, recv):
        first, size = splits[part]
        cut = pl.ds(first, size)
        peer = jnp.bitwise_xor(me, offset)
        return remote(
            source.at[rows_of(peer), cut],
            target.at[rows_of(me), cut],
            offset,
            send.at[part, offset],
            recv.at[part, offset],
        )

    for part, (first, size) in enumerate(splits):

        def activate(tile, carry, first=first):
            at = pl.ds(pl.multiple_of(first + tile * 128, 128), 128)
            gate = gate_acc[:, at] * gate_scale[:, at]
            up = up_acc[:, at] * up_scale[:, at]
            hid[:, at] = (gate / (1.0 + jnp.exp(-gate)) * up).astype(BF16)
            return carry

        lax.fori_loop(0, size // 128, activate, 0)
        each_peer(lambda j, part=part: exchange(hid, arrived, part, j, hid_send, hid_recv).start())
    odd_pad[...] = jnp.zeros_like(odd_pad)
    odd_pad[0:odd_order, 0:odd_order] = odd[...]
    for copy in constant_copies:
        copy.wait()

    def build(tile, carry):
        at = pl.ds(pl.multiple_of(tile * 128, 128), 128)
        factor_rows = lax.dot_general(
                ones_row[at, :], odd_pad[...].astype(BF16), (((1,), (1,)), ((), ())), preferred_element_type=F32
            ).astype(BF16)
        factor = jnp.dot(factor_rows, ones_col[...], preferred_element_type=F32)
        signs = jnp.dot(sign_row[at, :], sign_col[...], preferred_element_type=F32)
        mixer[at, :] = (factor * signs).astype(BF16)
        return carry

    lax.fori_loop(0, width // 128, build, 0)
    arrived[rows_of(me), :] = hid[rows_of(me), :]
    for part in range(len(splits)):
        each_peer(lambda j, part=part: exchange(hid, arrived, part, j, hid_send, hid_recv).wait_recv())

    def mix(first, size):
        at = pl.ds(first, size)
        flat = jnp.dot(arrived[...], mixer[:, at], preferred_element_type=F32)
        terms = [flat[i * share : (i + 1) * share] for i in range(n)]
        bit = 1
        while bit < n:
            terms = [
                terms[i ^ bit] - terms[i] if i & bit else terms[i] + terms[i ^ bit] for i in range(n)
            ]
            bit *= 2
        for i in range(n):
            rot_out[i * share : (i + 1) * share, at] = (terms[i] * walsh_scale).astype(BF16)

    for part, (first, size) in enumerate(splits):

        def mix_tile(tile, carry, first=first):
            mix(pl.multiple_of(first + tile * 256, 256), 256)
            return carry

        lax.fori_loop(0, size // 256, mix_tile, 0)
        if size % 256:
            mix(first + size // 256 * 256, size % 256)
        each_peer(lambda j, part=part: exchange(rot_out, rot_in, part, j, rot_send, rot_recv).start())
    rot_in[rows_of(me), :] = rot_out[rows_of(me), :]
    for part in range(len(splits)):
        each_peer(lambda j, part=part: exchange(rot_out, rot_in, part, j, rot_send, rot_recv).wait_recv())

    groups = steps // 2

    def down_block(step):
        down_copy(step).wait()
        value = jnp.dot(rot_in[...], down_w[lax.rem(step, DOWN_RING)], preferred_element_type=F32)
        return value

    def refill(step):
        @pl.when(step + DOWN_RING < steps)
        def _():
            down_copy(step + DOWN_RING).start()

    def to_core(group):
        return remote(core_out.at[group], core_in.at[group], 1, core_send.at[group], core_recv.at[group])

    def to_x(turn):
        return remote(x_out.at[turn], x_in.at[turn], 2, x_send.at[turn], x_recv.at[turn])

    def to_z(turn, offset):
        return remote(z_out.at[turn], z_in.at[turn], offset, z_send.at[turn], z_recv.at[turn])

    def combine(group):
        to_core(group).wait_recv()
        total = kept[group] + core_in[group].astype(F32)
        turn = group // 2

        @pl.when(group % 2 == 0)
        def _():
            x_out[turn] = total.astype(BF16)
            to_x(turn).start()

        @pl.when(group % 2 == 1)
        def _():
            kept[group] = total

    def lower(group, carry):
        core_out[group] = down_block(2 * group).astype(BF16)
        to_core(group).start()
        refill(2 * group)
        kept[group] = down_block(2 * group + 1)
        refill(2 * group + 1)

        @pl.when(group > 0)
        def _():
            combine(group - 1)

        return carry

    lax.fori_loop(0, groups, lambda g, c: lower(jnp.int32(g), c), 0)
    combine(jnp.int32(groups - 1))

    to_x(0).wait_recv()
    z_out[0] = (kept[1] + x_in[0].astype(F32)).astype(BF16)
    to_z(0, 4).start()
    to_x(1).wait_recv()
    to_z(0, 4).wait_recv()
    z_out[1] = (kept[3] + x_in[1].astype(F32) + z_in[0].astype(F32)).astype(BF16)
    to_z(1, 8).start()
    to_x(2).wait_recv()
    z_out[2] = (kept[5] + x_in[2].astype(F32)).astype(BF16)
    to_z(2, 4).start()
    to_x(3).wait_recv()
    to_z(1, 8).wait_recv()
    total = kept[7] + x_in[3].astype(F32) + z_in[1].astype(F32)
    to_z(2, 4).wait_recv()
    out[...] = ((total + z_in[2].astype(F32)) * down_scale[...]).astype(BF16)

    for moves in ONWARD:
        for block, offset in moves:
            pass_on(block, offset).wait_send()
    each_peer(lambda j: sums_to(j).wait_send())
    for part in range(len(splits)):
        each_peer(lambda j, part=part: exchange(hid, arrived, part, j, hid_send, hid_recv).wait_send())
        each_peer(lambda j, part=part: exchange(rot_out, rot_in, part, j, rot_send, rot_recv).wait_send())

    def finish(group, carry):
        to_core(group).wait_send()
        return carry

    lax.fori_loop(0, groups, finish, 0)
    for turn in range(4):
        to_x(turn).wait_send()
    for turn, offset in ((0, 4), (1, 8), (2, 4)):
        to_z(turn, offset).wait_send()


def small_signs(order):
    indices = np.arange(order)
    common = indices[:, None] & indices[None, :]
    parity = np.zeros_like(common)
    while common.any():
        parity ^= common & 1
        common >>= 1
    return 1.0 - 2.0 * parity


def fused_shards(
    tokens,
    norm_gain,
    gate_levels,
    gate_scale,
    up_levels,
    up_scale,
    odd_factor,
    down_levels,
    down_scale,
):
    n = lax.axis_size("tensor")
    rows, depth = tokens.shape
    width = gate_levels.shape[1]
    odd_order = odd_factor.shape[0]
    order = width // odd_order
    units = np.arange(width)
    ones = np.zeros((width, 128), np.float32)
    ones[units, units % odd_order] = 1.0
    owners = np.zeros((width, order), np.float32)
    owners[units, units // odd_order] = 1.0
    signs = owners @ small_signs(order)
    constants = [jnp.asarray(a, BF16) for a in (ones, ones.T, signs, owners.T)]
    half = width // 2 // 256 * 256
    splits = ((0, half), (half, width - half))
    vmem = pl.BlockSpec(memory_space=pltpu.VMEM)
    hbm = pl.BlockSpec(memory_space=pl.ANY)
    dma = pltpu.SemaphoreType.DMA
    block = (rows, depth)
    kernel = functools.partial(fused_kernel, n, odd_order, splits, 1.0 / math.sqrt(order * n))
    return pl.pallas_call(
        kernel,
        out_shape=jax.ShapeDtypeStruct(block, BF16),
        in_specs=[vmem, vmem, hbm, vmem, hbm, vmem, vmem, hbm, vmem] + [hbm] * 4,
        out_specs=vmem,
        scratch_shapes=[
            pltpu.VMEM((n,) + block, BF16),
            pltpu.VMEM((rows, 128), F32),
            pltpu.VMEM((1, width), F32),
            pltpu.VMEM((1, width), F32),
            pltpu.VMEM((n, 8, rows), F32),
            pltpu.VMEM((128, 128), F32),
            pltpu.VMEM((width, 128), BF16),
            pltpu.VMEM((128, width), BF16),
            pltpu.VMEM((width, 128), BF16),
            pltpu.VMEM((128, width), BF16),
            pltpu.VMEM((RING, depth, width), BF16),
            pltpu.VMEM((RING, depth, width), BF16),
            pltpu.VMEM((DOWN_RING, width, depth), BF16),
            pltpu.VMEM((rows, width), F32),
            pltpu.VMEM((rows, width), F32),
            pltpu.VMEM((width, width), BF16),
            pltpu.VMEM((rows, width), BF16),
            pltpu.VMEM((rows, width), BF16),
            pltpu.VMEM((rows, width), BF16),
            pltpu.VMEM((rows, width), BF16),
            pltpu.VMEM((8,) + block, F32),
            pltpu.VMEM((8,) + block, BF16),
            pltpu.VMEM((8,) + block, BF16),
            pltpu.VMEM((4,) + block, BF16),
            pltpu.VMEM((4,) + block, BF16),
            pltpu.VMEM((3,) + block, BF16),
            pltpu.VMEM((3,) + block, BF16),
            dma((RING,)),
            dma((RING,)),
            dma((DOWN_RING,)),
            dma((n,)),
            dma((n,)),
            dma((4,)),
            dma((n,)),
            dma((n,)),
            dma((2, n)),
            dma((2, n)),
            dma((2, n)),
            dma((2, n)),
            dma((8,)),
            dma((8,)),
            dma((4,)),
            dma((4,)),
            dma((3,)),
            dma((3,)),
        ],
        compiler_params=pltpu.CompilerParams(
            collective_id=0, has_side_effects=True, vmem_limit_bytes=64 * 1024 * 1024 - 65536
        ),
        cost_estimate=pl.CostEstimate(
            flops=2 * rows * width * (3 * n * depth + width),
            bytes_accessed=6 * n * depth * width,
            transcendentals=rows * width,
        ),
    )(
        tokens,
        norm_gain.reshape(n, 1, depth),
        gate_levels,
        gate_scale,
        up_levels,
        up_scale,
        odd_factor,
        down_levels,
        down_scale.reshape(1, depth),
        *constants,
    )


def partner_2(block, axis, distance):
    count = lax.axis_size(axis)
    route = []
    for low in range(count):
        high = low | 1 << distance
        if high != low and high < count:
            route += [(low, high), (high, low)]
    return lax.ppermute(block, axis, route)


def sign_table(order):
    indices = jnp.arange(order, dtype=jnp.int32)
    common_bits = jnp.bitwise_and(indices[:, None], indices[None, :])
    parity = jnp.zeros((order, order), jnp.int32)
    for bit_index in range(max(1, order.bit_length())):
        parity = parity + jnp.bitwise_and(jnp.right_shift(common_bits, bit_index), 1)
    return (1 - 2 * jnp.bitwise_and(parity, 1)).astype(jnp.float32)


def shards(
    tokens,
    norm_gain,
    gate_levels,
    gate_scale,
    up_levels,
    up_scale,
    odd_factor,
    down_levels,
    down_scale,
):
    devices = lax.axis_size("tensor")
    order = gate_levels.shape[1] // odd_factor.shape[0]
    if devices == 16 and order == 128 and tokens.shape[1] % 128 == 0 and tokens.shape[0] % 256 == 0:
        return fused_shards(
            tokens,
            norm_gain,
            gate_levels,
            gate_scale,
            up_levels,
            up_scale,
            odd_factor,
            down_levels,
            down_scale,
        )
    gathered = lax.all_gather(tokens, "tensor", axis=1, tiled=True)
    floats = gathered.astype(jnp.float32)
    inverse = lax.rsqrt(jnp.mean(floats * floats, axis=1, keepdims=True) + 1e-05)
    normed = (floats * inverse * norm_gain).astype(jnp.bfloat16)
    gate_out = jnp.dot(normed, gate_levels, preferred_element_type=jnp.float32) * gate_scale
    up_out = jnp.dot(normed, up_levels, preferred_element_type=jnp.float32) * up_scale
    hidden = (jax.nn.silu(gate_out) * up_out).astype(jnp.bfloat16)
    odd_order = odd_factor.shape[0]
    hidden_width = hidden.shape[1]
    local_order = hidden_width // odd_order
    local_mixer = jnp.kron(sign_table(local_order), odd_factor.T)
    spread = jnp.dot(hidden.astype(jnp.float32), local_mixer, precision=lax.Precision.HIGHEST)
    position = lax.axis_index("tensor")
    for bit_index in range(devices.bit_length() - 1):
        partner = partner_2(spread, "tensor", bit_index)
        is_upper = jnp.bitwise_and(jnp.right_shift(position, bit_index), 1) == 1
        spread = jnp.where(is_upper, partner - spread, spread + partner)
    walsh_scale = 1.0 / math.sqrt(local_order * devices)
    rotated = (spread * walsh_scale).astype(jnp.bfloat16)
    partials = jnp.dot(rotated, down_levels, preferred_element_type=jnp.float32)
    summed = lax.psum_scatter(partials, "tensor", scatter_dimension=1, tiled=True)
    return (summed * down_scale).astype(jnp.bfloat16)


def solution(mesh):
    placed = (
        P("group", "tensor"),
        P(),
        P(None, "tensor"),
        P("tensor"),
        P(None, "tensor"),
        P("tensor"),
        P(),
        P("tensor", None),
        P("tensor"),
    )
    return jax.shard_map(
        shards, mesh=mesh, in_specs=placed, out_specs=P("group", "tensor"), check_vma=False
    )
```
